32 devices in a mesh: surveys: 2 (over y), tx: 4 (over z), ty: 4 (over x, core).
Axes of the slice: x: 2, y: 2, z: 4, core: 2. Of those that a mesh axis runs over, the one named last changes fastest.
Arguments:
- model_pert: bfloat16 [64, 64, 1024], P('surveys', 'tx', 'ty'), parts along dimension 0, may hold values from -6 to 6
- station_cells: int32 [8, 4, 512], P(('surveys', 'tx'), 'ty'), parts along dimension 0, may hold values from 0 to 4095, as said below
- station_resid: bfloat16 [8, 4, 48, 512], P(('surveys', 'tx'), 'ty'), parts along dimension 0, may hold values from -6 to 6
- data_weight: int32 [8, 4, 48, 512], P(('surveys', 'tx'), 'ty'), parts along dimension 0, may hold values 0 or 1
- kernels: bfloat16 [48, 32, 9, 9], replicated, may hold values from -0.125 to 0.125
Outputs:
- predicted: float32 [8, 4, 48, 512], P(('surveys', 'tx'), 'ty'), parts along dimension 0
- gradient: float32 [64, 64, 1024], P('surveys', 'tx', 'ty'), parts along dimension 0
The draws below stay inside these ranges and needn't reach their ends.
There are 2 independent parts, one for each index of `surveys`. The reference program is written for one: setup_inputs(seed, part) draws one part's arguments, and reference() takes and returns one part's arrays. A program takes and returns all parts, laid end to end along the dimension named above; an argument that names none is the same for every part. Nothing has to cross between parts.
Inputs may be any that keep to these rules, and one draw needn't show every extreme that they name: `station_cells`: within one tile the 512 station indices are distinct; every tile has a station at its first cell and one at its last cell.
All inputs are finite; a program needn't handle non-finite values. No bound on the sum of `data_weight` on one device may be relied on, other than what follows from the above.
Results may differ from the reference program's by a relative error of at most 0.0003.
Values may be sent and summed in bfloat16 or wider, within the bound.
A program may use at most 64 MiB of HBM per device.

```python
import jax
import jax.numpy as jnp
from jax import lax

L = 32
K = 48
CX = 16
CY = 256
S_DEV = 512
TROWS = 4
TCOLS = 4
NX = 64
NY = 1024


def draw_stations_tile(tile_key):
    first_key, second_key = jax.random.split(tile_key)
    cell_total = CX * CY
    inner = jax.random.permutation(first_key, cell_total - 2).astype(jnp.int32) + 1
    chosen = jnp.concatenate([jnp.array([0, cell_total - 1], jnp.int32), inner[:S_DEV - 2]])
    order = jax.random.permutation(second_key, S_DEV)
    return chosen[order].astype(jnp.int32)


def draw_station_cells(key, part):
    tile_keys = jax.random.split(jax.random.fold_in(key, 7), TROWS * TCOLS)
    return jax.vmap(draw_stations_tile)(tile_keys).reshape(TROWS, TCOLS, S_DEV).astype(jnp.int32)


def set_ends(drawn, stream_key, low, high):
    spot = [jax.random.randint(jax.random.fold_in(stream_key, axis), (), 0, length) for axis, length in enumerate(drawn.shape)]
    widest = drawn.shape.index(max(drawn.shape))
    neighbour = spot[:widest] + [(spot[widest] + 1) % drawn.shape[widest]] + spot[widest + 1:]
    return drawn.at[tuple(spot)].set(low).at[tuple(neighbour)].set(high)


def level_of(own_key, extent, shards, least, high):
    level, own = 1.0, jax.random.fold_in(own_key, 6)
    for dim, parts in shards:
        heights = jnp.exp(jax.random.uniform(jax.random.fold_in(own, dim), (parts,), jnp.float32, least / len(shards), high / len(shards)))
        level = level * jnp.repeat(heights, extent[dim] // parts).reshape([-1 if axis == dim else 1 for axis in range(len(extent))])
    return level


def bell_draw(rng, shape, width, most, shards=(), held_as=jnp.bfloat16):
    entries = jax.random.normal(rng, shape, jnp.float32) * width
    if len(shards) > 0:
        entries = level_of(rng, shape, shards, -0.22, 0.18) * entries
    return jnp.clip(entries, min=-most, max=most).astype(held_as)


def setup_inputs(seed: int = 0, part: int = 0) -> dict:
    streams_of = jax.random.split(jax.random.key(seed), 6)
    own_keys = jax.random.split(jax.random.fold_in(streams_of[5], part), 6)
    return {
        "model_pert": bell_draw(own_keys[0], (L, NX, NY), 1.0, 6.0, ((1, 4), (2, 4))),
        "station_cells": draw_station_cells(jax.random.fold_in(jax.random.fold_in(streams_of[5], part), 71), part),
        "station_resid": bell_draw(own_keys[2], (TROWS, TCOLS, K, S_DEV), 1.0, 6.0, ((0, 4), (1, 4))),
        "data_weight": set_ends((jax.random.randint(own_keys[3], (TROWS, TCOLS, K, S_DEV), 0, 4) < 3).astype(jnp.int32), jax.random.fold_in(own_keys[3], 1), 0, 1),
        "kernels": bell_draw(streams_of[4], (K, L, 9, 9), (L * 81) ** -0.5, 0.125),
    }


def correlate(field, weights):
    return lax.conv_general_dilated(field[None], weights, (1, 1), ((4, 4), (4, 4)), dimension_numbers=("NCHW", "OIHW", "NCHW"), precision=lax.Precision.HIGHEST)[0]


def reference(model_pert, station_cells, station_resid, data_weight, kernels):
    tile_row = jnp.arange(TROWS, dtype=jnp.int32)[:, None, None]
    tile_col = jnp.arange(TCOLS, dtype=jnp.int32)[None, :, None]
    grid_row = tile_row * CX + station_cells // CY
    grid_col = tile_col * CY + station_cells % CY
    flat_index = (grid_row * NY + grid_col).reshape(-1).astype(jnp.int32)
    weights_float = data_weight.astype(jnp.float32)
    weighted = (station_resid.astype(jnp.float32) * weights_float).astype(jnp.bfloat16)
    weighted = jnp.transpose(weighted, (2, 0, 1, 3)).reshape(K, -1)
    resid_grid = jnp.zeros((K, NX * NY), jnp.bfloat16).at[:, flat_index].set(weighted).reshape(K, NX, NY)
    kernel_float = kernels.astype(jnp.float32)
    field = correlate(model_pert.astype(jnp.float32), kernel_float)
    sampled = field.reshape(K, NX * NY)[:, flat_index].reshape(K, TROWS, TCOLS, S_DEV)
    predicted = jnp.transpose(sampled, (1, 2, 0, 3)) * weights_float
    flipped = jnp.transpose(kernel_float, (1, 0, 2, 3))[:, :, ::-1, ::-1]
    gradient = correlate(resid_grid.astype(jnp.float32), flipped)
    return predicted, gradient
```

```python
import functools

import jax
import jax.numpy as jnp
from jax import lax
from jax.experimental import pallas as pl
from jax.experimental.pallas import tpu as pltpu
from jax.sharding import PartitionSpec as P

HALO = 4
TAPS = 9
LANES = 128
EDGE = 16
BF16 = jnp.bfloat16
F32 = jnp.float32
NT = (((1,), (1,)), ((), ()))


def dot_nt(a, b):
    return lax.dot_general(a, b, NT, preferred_element_type=F32)


def dot_nn(a, b):
    return jnp.dot(a, b, preferred_element_type=F32)


def spread_rows(values, station_rows, first, count):
    return jnp.concatenate(
        [jnp.where(station_rows == first + x, values, 0.0).astype(BF16) for x in range(count)],
        axis=0,
    )


def one_hot(ids, count, first=0):
    spot = lax.broadcasted_iota(jnp.int32, (count, ids.shape[1]), 0) + first
    return jnp.where(spot == ids, 1.0, 0.0).astype(BF16)


def exchange_kernel(
    dims,
    cells_ref,
    resid_ref,
    weight_ref,
    model_ref,
    own_model,
    halo_model,
    halo_resid,
    halo_cells,
    edges,
    corners,
    send_resid,
    send_cells,
    send_edges,
    send_sems,
    recv_sems,
):
    tx_count, ty_count, layers, resps, rows, cols = dims
    tx, ty = lax.axis_index("tx"), lax.axis_index("ty")
    has = {-1: tx > 0, 1: tx < tx_count - 1}
    has_col = {-1: ty > 0, 1: ty < ty_count - 1}
    around = [(dx, dy) for dx in (-1, 0, 1) for dy in (-1, 0, 1) if (dx, dy) != (0, 0)]

    def exists(dx, dy):
        ok = None
        for part in ([has[dx]] if dx else []) + ([has_col[dy]] if dy else []):
            ok = part if ok is None else jnp.logical_and(ok, part)
        return ok

    barrier = pltpu.get_barrier_semaphore()
    for dx, dy in around:
        @pl.when(exists(dx, dy))
        def _():
            pl.semaphore_signal(
                barrier,
                inc=1,
                device_id={"tx": tx + dx, "ty": ty + dy},
                device_id_type=pl.DeviceIdType.MESH,
            )

    weighted = resid_ref[...].astype(F32) * weight_ref[...].astype(F32)
    send_resid[...] = weighted.astype(BF16)
    send_cells[...] = jnp.broadcast_to(cells_ref[...], send_cells.shape)

    total = layers * rows
    to = lax.broadcasted_iota(jnp.int32, (total, total), 0)
    frm = lax.broadcasted_iota(jnp.int32, (total, total), 1)
    source = (to % layers) * rows + to // layers
    perm = jnp.where(frm == source, 1.0, 0.0).astype(BF16)
    own_model[...] = dot_nn(perm, model_ref[...]).astype(BF16)

    cells = cells_ref[...]
    row_of, col_of = cells // cols, cells % cols
    spread = spread_rows(weighted, row_of, 0, rows)
    near = lax.broadcasted_iota(jnp.int32, (EDGE, cols), 0)
    lane = lax.broadcasted_iota(jnp.int32, (EDGE, cols), 1)
    for side, first in enumerate((0, cols - EDGE)):
        pick = jnp.where(lane == near + first, 1.0, 0.0).astype(BF16)
        send_edges[side, :, :total] = dot_nt(pick, own_model[...]).astype(BF16)
        send_edges[side, :, total:] = dot_nt(one_hot(col_of, EDGE, first), spread).astype(BF16)

    for side, dx in enumerate((-1, 1)):
        @pl.when(jnp.logical_not(has[dx]))
        def _():
            halo_model[side] = jnp.zeros(halo_model.shape[1:], BF16)
            halo_resid[side] = jnp.zeros(halo_resid.shape[1:], BF16)
            halo_cells[side] = jnp.zeros(halo_cells.shape[1:], jnp.int32)
    for side, dy in enumerate((-1, 1)):
        @pl.when(jnp.logical_not(has_col[dy]))
        def _():
            edges[side] = jnp.zeros(edges.shape[1:], BF16)
    for vert, dx in enumerate((-1, 1)):
        for side, dy in enumerate((-1, 1)):
            @pl.when(jnp.logical_not(exists(dx, dy)))
            def _():
                corners[vert, side] = jnp.zeros(corners.shape[2:], BF16)

    spans = [
        1 + both[-1].astype(jnp.int32) + both[1].astype(jnp.int32) for both in (has, has_col)
    ]
    pl.semaphore_wait(barrier, spans[0] * spans[1] - 1)

    thick = HALO * layers
    wide = corners.shape[-1] - thick

    def copies(dx, dy):
        pairs = []
        if dy == 0:
            mine = 1 if dx == -1 else 0
            start = 0 if dx == -1 else total - thick
            pairs.append((own_model.at[pl.ds(start, thick)], halo_model.at[mine]))
            pairs.append((send_resid, halo_resid.at[mine]))
            pairs.append((send_cells, halo_cells.at[mine]))
        elif dx == 0:
            mine = 1 if dy == -1 else 0
            pairs.append((send_edges.at[1 - mine], edges.at[mine]))
        else:
            vert, side = (1 if dx == -1 else 0), (1 if dy == -1 else 0)
            start = 0 if dx == -1 else total - thick
            start_resid = total if dx == -1 else send_edges.shape[-1] - wide
            src = send_edges.at[1 - side]
            dst = corners.at[vert, side]
            pairs.append((src.at[:, pl.ds(start, thick)], dst.at[:, pl.ds(0, thick)]))
            pairs.append((src.at[:, pl.ds(start_resid, wide)], dst.at[:, pl.ds(thick, wide)]))
        return pairs

    number = {}
    for d in around:
        for c in range(len(copies(*d))):
            number[d, c] = len(number)

    def remote(d, c):
        src, dst = copies(*d)[c]
        return pltpu.make_async_remote_copy(
            src_ref=src,
            dst_ref=dst,
            send_sem=send_sems.at[number[d, c]],
            recv_sem=recv_sems.at[number[d, c]],
            device_id={"tx": tx + d[0], "ty": ty + d[1]},
            device_id_type=pl.DeviceIdType.MESH,
        )

    order = sorted(around, key=lambda d: abs(d[1]))
    for d in order:
        @pl.when(exists(*d))
        def _():
            for c in range(len(copies(*d))):
                remote(d, c).start()
    for d in order:
        @pl.when(exists(*d))
        def _():
            for c in range(len(copies(*d))):
                remote(d, c).wait_send()

        @pl.when(exists(-d[0], -d[1]))
        def _():
            for c in range(len(copies(*d))):
                remote(d, c).wait_recv()


def product_kernel(
    dims,
    cells_ref,
    resid_ref,
    weight_ref,
    own_model,
    halo_model,
    halo_resid,
    halo_cells,
    edges,
    corners,
    forward_ref,
    adjoint_ref,
    predicted_ref,
    gradient_ref,
    padded_f,
    padded_a,
    stack_f,
    stack_a,
    tall_f,
    tall_a,
    toeplitz_f,
    toeplitz_a,
    mixed,
):
    tx_count, ty_count, layers, resps, rows, cols = dims
    tall = rows + 2 * HALO

    def toeplitz(taps_ref, long_ref, out_ref, depth, outs):
        step = TAPS * depth
        gap = (HALO - 1) * step
        size = taps_ref.shape[0]
        long_ref[pl.ds(0, gap), :] = jnp.zeros((gap, outs), BF16)
        long_ref[pl.ds(gap, size), :] = taps_ref[...]
        long_ref[pl.ds(gap + size, gap), :] = jnp.zeros((gap, outs), BF16)
        eye = jnp.where(
            lax.broadcasted_iota(jnp.int32, (outs, outs), 0)
            == lax.broadcasted_iota(jnp.int32, (outs, outs), 1),
            1.0,
            0.0,
        ).astype(BF16)
        width = out_ref.shape[1]
        for a in range(HALO):
            rolled = long_ref[pl.ds(gap - a * step, width), :]
            out_ref[pl.ds(a * outs, outs), :] = dot_nt(eye, rolled).astype(BF16)

    toeplitz(forward_ref, tall_f, toeplitz_f, layers, resps)
    toeplitz(adjoint_ref, tall_a, toeplitz_a, resps, layers)

    weights = weight_ref[...].astype(F32)
    weighted = resid_ref[...].astype(F32) * weights
    cells = cells_ref[...]
    row_of, col_of = cells // cols, cells % cols
    hot = one_hot(col_of, cols)

    total = layers * rows
    thick = HALO * layers
    padded_f[pl.ds(0, thick), LANES : LANES + cols] = halo_model[0]
    padded_f[pl.ds(thick, total), LANES : LANES + cols] = own_model[...]
    padded_f[pl.ds(thick + total, thick), LANES : LANES + cols] = halo_model[1]
    thick_a = HALO * resps
    total_a = resps * rows
    padded_a[pl.ds(thick_a, total_a), LANES : LANES + cols] = dot_nt(
        spread_rows(weighted, row_of, 0, rows), hot
    ).astype(BF16)
    for side in range(2):
        other = halo_cells[side][:1]
        values = halo_resid[side].astype(F32)
        first = rows - HALO if side == 0 else 0
        start = 0 if side == 0 else thick_a + total_a
        padded_a[pl.ds(start, thick_a), LANES : LANES + cols] = dot_nt(
            spread_rows(values, other // cols, first, HALO), one_hot(other % cols, cols)
        ).astype(BF16)
    for side in range(2):
        top, mid, low = corners[0, side], edges[side], corners[1, side]
        line_f = jnp.concatenate([top[:, :thick], mid[:, :total], low[:, :thick]], axis=1)
        wide = corners.shape[-1] - thick
        over = wide - thick_a
        line_a = jnp.concatenate(
            [top[:, thick + over :], mid[:, total:], low[:, thick : thick + thick_a]], axis=1
        )
        for line, padded in ((line_f, padded_f), (line_a, padded_a)):
            blank = jnp.zeros((LANES - EDGE, line.shape[1]), F32)
            line = line.astype(F32)
            if side == 0:
                block = jnp.concatenate([blank, line], axis=0).T
                padded[:, :LANES] = block.astype(BF16)
            else:
                block = jnp.concatenate([line, blank], axis=0).T
                padded[:, LANES + cols :] = block.astype(BF16)

    for padded, stack, depth in ((padded_f, stack_f, layers), (padded_a, stack_a, resps)):
        for x in range(tall):
            block = padded[pl.ds(x * depth, depth), :]
            for q in range(TAPS):
                begin = LANES - HALO + q
                stack[pl.ds((x * TAPS + q) * depth, depth), :] = block[:, begin : begin + cols]

    sampled = None
    for h in range(rows // HALO):
        deep = toeplitz_f.shape[1]
        field = dot_nn(toeplitz_f[...], stack_f[pl.ds(h * HALO * TAPS * layers, deep), :])
        high = field.astype(BF16)
        low = (field - high.astype(F32)).astype(BF16)
        spots = dot_nn(high, hot) + dot_nn(low, hot)
        for a in range(HALO):
            term = jnp.where(row_of == h * HALO + a, spots[a * resps : (a + 1) * resps], 0.0)
            sampled = term if sampled is None else sampled + term
    predicted_ref[...] = sampled * weights

    for h in range(rows // HALO):
        deep = toeplitz_a.shape[1]
        grad = dot_nn(toeplitz_a[...], stack_a[pl.ds(h * HALO * TAPS * resps, deep), :])
        for a in range(HALO):
            for t in range(cols // LANES):
                mixed[t, pl.ds(h * HALO + a, layers, stride=rows), :] = grad[
                    a * layers : (a + 1) * layers, t * LANES : (t + 1) * LANES
                ]
    for t in range(cols // LANES):
        gradient_ref[:, t * LANES : (t + 1) * LANES] = mixed[t]


def shards(tx_count, ty_count, model_pert, station_cells, station_resid, data_weight, kernels):
    layers, rows, cols = model_pert.shape
    resps = kernels.shape[0]
    stations = station_cells.shape[-1]
    dims = (tx_count, ty_count, layers, resps, rows, cols)
    cells, resid, weight = station_cells[0], station_resid[0, 0], data_weight[0, 0]
    model = model_pert.reshape(layers * rows, cols)
    line = (layers + resps) * rows
    thick_a = -(-HALO * resps // LANES) * LANES
    vmem = pl.BlockSpec(memory_space=pltpu.VMEM)
    shape = jax.ShapeDtypeStruct
    copy_count = 2 * 3 + 2 + 4 * 2
    exchanged = pl.pallas_call(
        functools.partial(exchange_kernel, dims),
        out_shape=(
            shape((layers * rows, cols), BF16),
            shape((2, HALO * layers, cols), BF16),
            shape((2, resps, stations), BF16),
            shape((2, 8, stations), jnp.int32),
            shape((2, EDGE, line), BF16),
            shape((2, 2, EDGE, HALO * layers + thick_a), BF16),
        ),
        in_specs=[vmem] * 4,
        out_specs=(vmem,) * 6,
        scratch_shapes=[
            pltpu.VMEM((resps, stations), BF16),
            pltpu.VMEM((8, stations), jnp.int32),
            pltpu.VMEM((2, EDGE, line), BF16),
            pltpu.SemaphoreType.DMA((copy_count,)),
            pltpu.SemaphoreType.DMA((copy_count,)),
        ],
        compiler_params=pltpu.CompilerParams(
            collective_id=0, has_side_effects=True, vmem_limit_bytes=24 * 2**20
        ),
    )(cells, resid, weight, model)

    forward = jnp.transpose(kernels, (2, 3, 1, 0)).reshape(TAPS * TAPS * layers, resps)
    adjoint = jnp.transpose(kernels[:, :, ::-1, ::-1], (2, 3, 0, 1))
    adjoint = adjoint.reshape(TAPS * TAPS * resps, layers)
    tall = rows + 2 * HALO
    reach = TAPS + HALO - 1
    predicted, gradient = pl.pallas_call(
        functools.partial(product_kernel, dims),
        out_shape=(
            shape((resps, stations), F32),
            shape((layers * rows, cols), F32),
        ),
        in_specs=[vmem] * 11,
        out_specs=(vmem,) * 2,
        scratch_shapes=[
            pltpu.VMEM((tall * layers, cols + 2 * LANES), BF16),
            pltpu.VMEM((tall * resps, cols + 2 * LANES), BF16),
            pltpu.VMEM((tall * TAPS * layers, cols), BF16),
            pltpu.VMEM((tall * TAPS * resps, cols), BF16),
            pltpu.VMEM(((TAPS + 2 * (HALO - 1)) * TAPS * layers, resps), BF16),
            pltpu.VMEM(((TAPS + 2 * (HALO - 1)) * TAPS * resps, layers), BF16),
            pltpu.VMEM((HALO * resps, reach * TAPS * layers), BF16),
            pltpu.VMEM((HALO * layers, reach * TAPS * resps), BF16),
            pltpu.VMEM((cols // LANES, layers * rows, LANES), F32),
        ],
        compiler_params=pltpu.CompilerParams(vmem_limit_bytes=40 * 2**20),
    )(cells, resid, weight, *exchanged, forward, adjoint)
    return predicted[None, None], gradient.reshape(layers, rows, cols)


def solution(mesh):
    placed = (
        P("surveys", "tx", "ty"),
        P(("surveys", "tx"), "ty", None),
        P(("surveys", "tx"), "ty", None, None),
        P(("surveys", "tx"), "ty", None, None),
        P(),
    )
    return jax.shard_map(
        functools.partial(shards, mesh.shape["tx"], mesh.shape["ty"]),
        mesh=mesh,
        in_specs=placed,
        out_specs=(P(("surveys", "tx"), "ty", None, None), P("surveys", "tx", "ty")),
        check_vma=False,
    )
```

```python
import functools
import math

import jax
import jax.numpy as jnp
from jax import lax
from jax.experimental import pallas as pl
from jax.experimental.pallas import tpu as pltpu
from jax.sharding import PartitionSpec as P

HALO = 4
TAPS = 9
LANES = 128
EDGE = 16
BF16 = jnp.bfloat16
F32 = jnp.float32
NT = (((1,), (1,)), ((), ()))


def dot_nt(a, b):
    return lax.dot_general(a, b, NT, preferred_element_type=F32)


def dot_nn(a, b):
    return jnp.dot(a, b, preferred_element_type=F32)


def spread_rows(values, station_rows, first, count):
    return jnp.concatenate(
        [jnp.where(station_rows == first + x, values, 0.0).astype(BF16) for x in range(count)],
        axis=0,
    )


def one_hot(ids, count, first=0):
    spot = lax.broadcasted_iota(jnp.int32, (count, ids.shape[1]), 0) + first
    return jnp.where(spot == ids, 1.0, 0.0).astype(BF16)


def round_up(size):
    return -(-size // LANES) * LANES


def offsets(depth):
    return round_up((HALO - 1) * TAPS * depth)


def exchange_kernel(
    dims,
    cells_hbm,
    resid_hbm,
    weight_hbm,
    model_hbm,
    taps_hbm,
    weight_ref,
    send_cells,
    own_resid,
    toeplitz_f,
    toeplitz_a,
    own_model,
    halo_model,
    halo_resid,
    halo_cells,
    edges,
    corners,
    cells_ref,
    resid_ref,
    model_ref,
    taps_ref,
    base_f,
    base_a,
    send_resid,
    send_edges,
    load_sems,
    send_sems,
    recv_sems,
):
    tx_count, ty_count, layers, resps, rows, cols = dims
    tx, ty = lax.axis_index("tx"), lax.axis_index("ty")
    has = {-1: tx > 0, 1: tx < tx_count - 1}
    has_col = {-1: ty > 0, 1: ty < ty_count - 1}
    around = [(dx, dy) for dx in (-1, 0, 1) for dy in (-1, 0, 1) if (dx, dy) != (0, 0)]

    def exists(dx, dy):
        ok = None
        for part in ([has[dx]] if dx else []) + ([has_col[dy]] if dy else []):
            ok = part if ok is None else jnp.logical_and(ok, part)
        return ok

    loads = [
        pltpu.make_async_copy(src, dst, load_sems.at[n])
        for n, (src, dst) in enumerate(
            (
                (cells_hbm, cells_ref),
                (resid_hbm, resid_ref),
                (weight_hbm, weight_ref),
                (model_hbm, model_ref),
                (taps_hbm, taps_ref),
            )
        )
    ]
    for load in loads:
        load.start()
    barrier = pltpu.get_barrier_semaphore()
    for dx, dy in around:
        @pl.when(exists(dx, dy))
        def _():
            pl.semaphore_signal(
                barrier,
                inc=1,
                device_id={"tx": tx + dx, "ty": ty + dy},
                device_id_type=pl.DeviceIdType.MESH,
            )

    for side, dx in enumerate((-1, 1)):
        @pl.when(jnp.logical_not(has[dx]))
        def _():
            halo_model[side] = jnp.zeros(halo_model.shape[1:], BF16)
            halo_resid[side] = jnp.zeros(halo_resid.shape[1:], BF16)
            halo_cells[side] = jnp.zeros(halo_cells.shape[1:], jnp.int32)
    for side, dy in enumerate((-1, 1)):
        @pl.when(jnp.logical_not(has_col[dy]))
        def _():
            edges[side] = jnp.zeros(edges.shape[1:], BF16)
    for vert, dx in enumerate((-1, 1)):
        for side, dy in enumerate((-1, 1)):
            @pl.when(jnp.logical_not(exists(dx, dy)))
            def _():
                corners[vert, side] = jnp.zeros(corners.shape[2:], BF16)

    for load in loads[:3]:
        load.wait()
    weighted = resid_ref[...].astype(F32) * weight_ref[...].astype(F32)
    send_resid[...] = weighted.astype(BF16)
    send_cells[...] = jnp.broadcast_to(cells_ref[...], send_cells.shape)

    total = layers * rows
    loads[3].wait()
    to = lax.broadcasted_iota(jnp.int32, (total, total), 0)
    frm = lax.broadcasted_iota(jnp.int32, (total, total), 1)
    source = (to % layers) * rows + to // layers
    perm = jnp.where(frm == source, 1.0, 0.0).astype(BF16)
    own_model[...] = dot_nn(perm, model_ref[...]).astype(BF16)

    spans = [
        1 + both[-1].astype(jnp.int32) + both[1].astype(jnp.int32) for both in (has, has_col)
    ]
    pl.semaphore_wait(barrier, spans[0] * spans[1] - 1)

    thick = HALO * layers
    wide = corners.shape[-1] - thick

    def copies(dx, dy):
        pairs = []
        if dy == 0:
            mine = 1 if dx == -1 else 0
            start = 0 if dx == -1 else total - thick
            pairs.append((own_model.at[pl.ds(start, thick)], halo_model.at[mine]))
            pairs.append((send_resid, halo_resid.at[mine]))
            pairs.append((send_cells, halo_cells.at[mine]))
        elif dx == 0:
            mine = 1 if dy == -1 else 0
            pairs.append((send_edges.at[1 - mine], edges.at[mine]))
        else:
            vert, side = (1 if dx == -1 else 0), (1 if dy == -1 else 0)
            start = 0 if dx == -1 else total - thick
            start_resid = total if dx == -1 else send_edges.shape[-1] - wide
            src = send_edges.at[1 - side]
            dst = corners.at[vert, side]
            pairs.append((src.at[:, pl.ds(start, thick)], dst.at[:, pl.ds(0, thick)]))
            pairs.append((src.at[:, pl.ds(start_resid, wide)], dst.at[:, pl.ds(thick, wide)]))
        return pairs

    number = {}
    for d in around:
        for c in range(len(copies(*d))):
            number[d, c] = len(number)

    def remote(d, c):
        src, dst = copies(*d)[c]
        return pltpu.make_async_remote_copy(
            src_ref=src,
            dst_ref=dst,
            send_sem=send_sems.at[number[d, c]],
            recv_sem=recv_sems.at[number[d, c]],
            device_id={"tx": tx + d[0], "ty": ty + d[1]},
            device_id_type=pl.DeviceIdType.MESH,
        )

    order = sorted(around, key=lambda d: abs(d[1]))

    def start(d):
        @pl.when(exists(*d))
        def _():
            for c in range(len(copies(*d))):
                remote(d, c).start()

    for d in order[:2]:
        start(d)

    cells = cells_ref[...]
    row_of, col_of = cells // cols, cells % cols
    spread = spread_rows(weighted, row_of, 0, rows)
    near = lax.broadcasted_iota(jnp.int32, (EDGE, cols), 0)
    lane = lax.broadcasted_iota(jnp.int32, (EDGE, cols), 1)
    for side, first in enumerate((0, cols - EDGE)):
        pick = jnp.where(lane == near + first, 1.0, 0.0).astype(BF16)
        send_edges[side, :, :total] = dot_nt(pick, own_model[...]).astype(BF16)
        send_edges[side, :, total:] = dot_nt(one_hot(col_of, EDGE, first), spread).astype(BF16)

    for d in order[2:]:
        start(d)

    own_resid[...] = dot_nt(spread, one_hot(col_of, cols)).astype(BF16)

    loads[4].wait()
    offset_f, offset_a = offsets(layers), offsets(resps)
    eye = jnp.where(
        lax.broadcasted_iota(jnp.int32, (resps, resps), 0)
        == lax.broadcasted_iota(jnp.int32, (resps, resps), 1),
        1.0,
        0.0,
    ).astype(BF16)
    base_f[...] = jnp.zeros_like(base_f)
    size_f = TAPS * TAPS * layers
    base_f[:, offset_f : offset_f + size_f] = dot_nt(eye, taps_ref[...]).astype(BF16)
    base_a[...] = jnp.zeros_like(base_a)
    group = LANES // math.gcd(LANES, resps)
    for lead in range(0, TAPS * TAPS, group):
        blocks = [
            taps_ref[pl.ds((TAPS * TAPS - 1 - m) * layers, layers), :]
            for m in range(lead, min(lead + group, TAPS * TAPS))
        ]
        begin = offset_a + lead * resps
        base_a[:, begin : begin + len(blocks) * resps] = jnp.concatenate(blocks, axis=1)
    for base, out, offset, depth in (
        (base_f, toeplitz_f, offset_f, layers),
        (base_a, toeplitz_a, offset_a, resps),
    ):
        height, width = base.shape[0], out.shape[1]
        whole = base[...]
        for a in range(HALO):
            begin = offset - a * TAPS * depth
            out[pl.ds(a * height, height), :] = whole[:, begin : begin + width]

    for d in order:
        @pl.when(exists(*d))
        def _():
            for c in range(len(copies(*d))):
                remote(d, c).wait_send()

        @pl.when(exists(-d[0], -d[1]))
        def _():
            for c in range(len(copies(*d))):
                remote(d, c).wait_recv()


def product_kernel(
    dims,
    weight_ref,
    cells_ref,
    own_resid,
    toeplitz_f,
    toeplitz_a,
    own_model,
    halo_model,
    halo_resid,
    halo_cells,
    edges,
    corners,
    predicted_ref,
    gradient_ref,
    padded_f,
    padded_a,
    stack_f,
    stack_a,
    mixed,
):
    tx_count, ty_count, layers, resps, rows, cols = dims
    tall = rows + 2 * HALO

    weights = weight_ref[...].astype(F32)
    cells = cells_ref[:1, :]
    row_of, col_of = cells // cols, cells % cols
    hot = one_hot(col_of, cols)

    total = layers * rows
    thick = HALO * layers
    padded_f[pl.ds(0, thick), LANES : LANES + cols] = halo_model[0]
    padded_f[pl.ds(thick, total), LANES : LANES + cols] = own_model[...]
    padded_f[pl.ds(thick + total, thick), LANES : LANES + cols] = halo_model[1]
    thick_a = HALO * resps
    total_a = resps * rows
    padded_a[pl.ds(thick_a, total_a), LANES : LANES + cols] = own_resid[...]
    for side in range(2):
        other = halo_cells[side][:1]
        values = halo_resid[side].astype(F32)
        first = rows - HALO if side == 0 else 0
        start = 0 if side == 0 else thick_a + total_a
        padded_a[pl.ds(start, thick_a), LANES : LANES + cols] = dot_nt(
            spread_rows(values, other // cols, first, HALO), one_hot(other % cols, cols)
        ).astype(BF16)
    for side in range(2):
        top, mid, low = corners[0, side], edges[side], corners[1, side]
        line_f = jnp.concatenate([top[:, :thick], mid[:, :total], low[:, :thick]], axis=1)
        wide = corners.shape[-1] - thick
        over = wide - thick_a
        line_a = jnp.concatenate(
            [top[:, thick + over :], mid[:, total:], low[:, thick : thick + thick_a]], axis=1
        )
        for line, padded in ((line_f, padded_f), (line_a, padded_a)):
            blank = jnp.zeros((LANES - EDGE, line.shape[1]), F32)
            line = line.astype(F32)
            if side == 0:
                block = jnp.concatenate([blank, line], axis=0).T
                padded[:, :LANES] = block.astype(BF16)
            else:
                block = jnp.concatenate([line, blank], axis=0).T
                padded[:, LANES + cols :] = block.astype(BF16)

    for padded, stack, depth in ((padded_f, stack_f, layers), (padded_a, stack_a, resps)):
        for x in range(tall):
            block = padded[pl.ds(x * depth, depth), :]
            for q in range(TAPS):
                begin = LANES - HALO + q
                stack[pl.ds((x * TAPS + q) * depth, depth), :] = block[:, begin : begin + cols]

    sampled = None
    for h in range(rows // HALO):
        deep = toeplitz_f.shape[1]
        field = dot_nn(toeplitz_f[...], stack_f[pl.ds(h * HALO * TAPS * layers, deep), :])
        high = field.astype(BF16)
        low = (field - high.astype(F32)).astype(BF16)
        spots = dot_nn(high, hot) + dot_nn(low, hot)
        for a in range(HALO):
            term = jnp.where(row_of == h * HALO + a, spots[a * resps : (a + 1) * resps], 0.0)
            sampled = term if sampled is None else sampled + term
    predicted_ref[...] = sampled * weights

    for h in range(rows // HALO):
        deep = toeplitz_a.shape[1]
        grad = dot_nn(toeplitz_a[...], stack_a[pl.ds(h * HALO * TAPS * resps, deep), :])
        for a in range(HALO):
            for t in range(cols // LANES):
                mixed[t, pl.ds(h * HALO + a, layers, stride=rows), :] = grad[
                    a * layers : (a + 1) * layers, t * LANES : (t + 1) * LANES
                ]
    for t in range(cols // LANES):
        gradient_ref[:, t * LANES : (t + 1) * LANES] = mixed[t]


def shards(tx_count, ty_count, model_pert, station_cells, station_resid, data_weight, kernels):
    layers, rows, cols = model_pert.shape
    resps = kernels.shape[0]
    stations = station_cells.shape[-1]
    dims = (tx_count, ty_count, layers, resps, rows, cols)
    cells, resid, weight = station_cells[0], station_resid[0, 0], data_weight[0, 0]
    model = model_pert.reshape(layers * rows, cols)
    line = (layers + resps) * rows
    thick_a = -(-HALO * resps // LANES) * LANES
    vmem = pl.BlockSpec(memory_space=pltpu.VMEM)
    shape = jax.ShapeDtypeStruct
    copy_count = 2 * 3 + 2 + 4 * 2
    hbm = pl.BlockSpec(memory_space=pltpu.HBM)
    reach = TAPS + HALO - 1
    wide_f, wide_a = reach * TAPS * layers, reach * TAPS * resps
    forward = jnp.transpose(kernels, (2, 3, 1, 0)).reshape(TAPS * TAPS * layers, resps)
    exchanged = pl.pallas_call(
        functools.partial(exchange_kernel, dims),
        out_shape=(
            shape((resps, stations), jnp.int32),
            shape((8, stations), jnp.int32),
            shape((resps * rows, cols), BF16),
            shape((HALO * resps, wide_f), BF16),
            shape((HALO * layers, wide_a), BF16),
            shape((layers * rows, cols), BF16),
            shape((2, HALO * layers, cols), BF16),
            shape((2, resps, stations), BF16),
            shape((2, 8, stations), jnp.int32),
            shape((2, EDGE, line), BF16),
            shape((2, 2, EDGE, HALO * layers + thick_a), BF16),
        ),
        in_specs=[hbm] * 5,
        out_specs=(vmem,) * 11,
        scratch_shapes=[
            pltpu.VMEM((1, stations), jnp.int32),
            pltpu.VMEM((resps, stations), BF16),
            pltpu.VMEM((layers * rows, cols), BF16),
            pltpu.VMEM((TAPS * TAPS * layers, resps), BF16),
            pltpu.VMEM((resps, round_up(offsets(layers) + wide_f)), BF16),
            pltpu.VMEM((layers, round_up(offsets(resps) + wide_a)), BF16),
            pltpu.VMEM((resps, stations), BF16),
            pltpu.VMEM((2, EDGE, line), BF16),
            pltpu.SemaphoreType.DMA((5,)),
            pltpu.SemaphoreType.DMA((copy_count,)),
            pltpu.SemaphoreType.DMA((copy_count,)),
        ],
        compiler_params=pltpu.CompilerParams(
            collective_id=0, has_side_effects=True, vmem_limit_bytes=24 * 2**20
        ),
    )(cells, resid, weight, model, forward)

    tall = rows + 2 * HALO
    predicted, gradient = pl.pallas_call(
        functools.partial(product_kernel, dims),
        out_shape=(
            shape((resps, stations), F32),
            shape((layers * rows, cols), F32),
        ),
        in_specs=[vmem] * 11,
        out_specs=(vmem,) * 2,
        scratch_shapes=[
            pltpu.VMEM((tall * layers, cols + 2 * LANES), BF16),
            pltpu.VMEM((tall * resps, cols + 2 * LANES), BF16),
            pltpu.VMEM((tall * TAPS * layers, cols), BF16),
            pltpu.VMEM((tall * TAPS * resps, cols), BF16),
            pltpu.VMEM((cols // LANES, layers * rows, LANES), F32),
        ],
        compiler_params=pltpu.CompilerParams(vmem_limit_bytes=32 * 2**20),
    )(*exchanged)
    return predicted[None, None], gradient.reshape(layers, rows, cols)


def solution(mesh):
    placed = (
        P("surveys", "tx", "ty"),
        P(("surveys", "tx"), "ty", None),
        P(("surveys", "tx"), "ty", None, None),
        P(("surveys", "tx"), "ty", None, None),
        P(),
    )
    return jax.shard_map(
        functools.partial(shards, mesh.shape["tx"], mesh.shape["ty"]),
        mesh=mesh,
        in_specs=placed,
        out_specs=(P(("surveys", "tx"), "ty", None, None), P("surveys", "tx", "ty")),
        check_vma=False,
    )
```

```python
import functools
import math

import jax
import jax.numpy as jnp
from jax import lax
from jax.experimental import pallas as pl
from jax.experimental.pallas import tpu as pltpu
from jax.sharding import PartitionSpec as P

HALO = 4
TAPS = 9
LANES = 128
EDGE = 16
BF16 = jnp.bfloat16
F32 = jnp.float32
NT = (((1,), (1,)), ((), ()))


def dot_nt(a, b):
    return lax.dot_general(a, b, NT, preferred_element_type=F32)


def dot_nn(a, b):
    return jnp.dot(a, b, preferred_element_type=F32)


def spread_rows(values, station_rows, first, count):
    return jnp.concatenate(
        [jnp.where(station_rows == first + x, values, 0.0).astype(BF16) for x in range(count)],
        axis=0,
    )


def one_hot(ids, count, first=0):
    spot = lax.broadcasted_iota(jnp.int32, (count, ids.shape[1]), 0) + first
    return jnp.where(spot == ids, 1.0, 0.0).astype(BF16)


def round_up(size):
    return -(-size // LANES) * LANES


def offsets(depth):
    return round_up((HALO - 1) * TAPS * depth)


def exchange_kernel(
    dims,
    cells_hbm,
    resid_hbm,
    weight_hbm,
    model_hbm,
    taps_hbm,
    weight_ref,
    send_cells,
    own_resid,
    toeplitz_f,
    toeplitz_a,
    own_model,
    halo_model,
    halo_resid,
    halo_cells,
    edges,
    corners,
    cells_ref,
    resid_ref,
    model_ref,
    taps_ref,
    base_f,
    base_a,
    send_resid,
    send_edges,
    load_sems,
    send_sems,
    recv_sems,
):
    tx_count, ty_count, layers, resps, rows, cols = dims
    tx, ty = lax.axis_index("tx"), lax.axis_index("ty")
    has = {-1: tx > 0, 1: tx < tx_count - 1}
    has_col = {-1: ty > 0, 1: ty < ty_count - 1}
    around = [(dx, dy) for dx in (-1, 0, 1) for dy in (-1, 0, 1) if (dx, dy) != (0, 0)]

    def exists(dx, dy):
        ok = None
        for part in ([has[dx]] if dx else []) + ([has_col[dy]] if dy else []):
            ok = part if ok is None else jnp.logical_and(ok, part)
        return ok

    loads = [
        pltpu.make_async_copy(src, dst, load_sems.at[n])
        for n, (src, dst) in enumerate(
            (
                (cells_hbm, cells_ref),
                (resid_hbm, resid_ref),
                (weight_hbm, weight_ref),
                (model_hbm, model_ref),
                (taps_hbm, taps_ref),
            )
        )
    ]
    for load in loads:
        load.start()
    barrier = pltpu.get_barrier_semaphore()
    for dx, dy in around:
        @pl.when(exists(dx, dy))
        def _():
            pl.semaphore_signal(
                barrier,
                inc=1,
                device_id={"tx": tx + dx, "ty": ty + dy},
                device_id_type=pl.DeviceIdType.MESH,
            )

    for side, dx in enumerate((-1, 1)):
        @pl.when(jnp.logical_not(has[dx]))
        def _():
            halo_model[side] = jnp.zeros(halo_model.shape[1:], BF16)
            halo_resid[side] = jnp.zeros(halo_resid.shape[1:], BF16)
            halo_cells[side] = jnp.zeros(halo_cells.shape[1:], jnp.int32)
    for side, dy in enumerate((-1, 1)):
        @pl.when(jnp.logical_not(has_col[dy]))
        def _():
            edges[side] = jnp.zeros(edges.shape[1:], BF16)
    for vert, dx in enumerate((-1, 1)):
        for side, dy in enumerate((-1, 1)):
            @pl.when(jnp.logical_not(exists(dx, dy)))
            def _():
                corners[vert, side] = jnp.zeros(corners.shape[2:], BF16)

    for load in loads[:3]:
        load.wait()
    weighted = resid_ref[...].astype(F32) * weight_ref[...].astype(F32)
    send_resid[...] = weighted.astype(BF16)
    send_cells[...] = jnp.broadcast_to(cells_ref[...], send_cells.shape)

    total = layers * rows
    loads[3].wait()
    to = lax.broadcasted_iota(jnp.int32, (total, total), 0)
    frm = lax.broadcasted_iota(jnp.int32, (total, total), 1)
    source = (to % layers) * rows + to // layers
    perm = jnp.where(frm == source, 1.0, 0.0).astype(BF16)
    own_model[...] = dot_nn(perm, model_ref[...]).astype(BF16)

    spans = [
        1 + both[-1].astype(jnp.int32) + both[1].astype(jnp.int32) for both in (has, has_col)
    ]
    pl.semaphore_wait(barrier, spans[0] * spans[1] - 1)

    thick = HALO * layers
    wide = corners.shape[-1] - thick

    def copies(dx, dy):
        pairs = []
        if dy == 0:
            mine = 1 if dx == -1 else 0
            start = 0 if dx == -1 else total - thick
            pairs.append((own_model.at[pl.ds(start, thick)], halo_model.at[mine]))
            pairs.append((send_resid, halo_resid.at[mine]))
            pairs.append((send_cells, halo_cells.at[mine]))
        elif dx == 0:
            mine = 1 if dy == -1 else 0
            pairs.append((send_edges.at[1 - mine], edges.at[mine]))
        else:
            vert, side = (1 if dx == -1 else 0), (1 if dy == -1 else 0)
            start = 0 if dx == -1 else total - thick
            start_resid = total if dx == -1 else send_edges.shape[-1] - wide
            src = send_edges.at[1 - side]
            dst = corners.at[vert, side]
            pairs.append((src.at[:, pl.ds(start, thick)], dst.at[:, pl.ds(0, thick)]))
            pairs.append((src.at[:, pl.ds(start_resid, wide)], dst.at[:, pl.ds(thick, wide)]))
        return pairs

    number = {}
    for d in around:
        for c in range(len(copies(*d))):
            number[d, c] = len(number)

    def remote(d, c):
        src, dst = copies(*d)[c]
        return pltpu.make_async_remote_copy(
            src_ref=src,
            dst_ref=dst,
            send_sem=send_sems.at[number[d, c]],
            recv_sem=recv_sems.at[number[d, c]],
            device_id={"tx": tx + d[0], "ty": ty + d[1]},
            device_id_type=pl.DeviceIdType.MESH,
        )

    order = sorted(around, key=lambda d: abs(d[1]))

    def start(d):
        @pl.when(exists(*d))
        def _():
            for c in range(len(copies(*d))):
                remote(d, c).start()

    for d in order[:2]:
        start(d)

    cells = cells_ref[...]
    row_of, col_of = cells // cols, cells % cols
    spread = spread_rows(weighted, row_of, 0, rows)
    near = lax.broadcasted_iota(jnp.int32, (EDGE, cols), 0)
    lane = lax.broadcasted_iota(jnp.int32, (EDGE, cols), 1)
    for side, first in enumerate((0, cols - EDGE)):
        pick = jnp.where(lane == near + first, 1.0, 0.0).astype(BF16)
        send_edges[side, :, :total] = dot_nt(pick, own_model[...]).astype(BF16)
        send_edges[side, :, total:] = dot_nt(one_hot(col_of, EDGE, first), spread).astype(BF16)

    for d in order[2:]:
        start(d)

    own_resid[...] = dot_nt(spread, one_hot(col_of, cols)).astype(BF16)

    loads[4].wait()
    offset_f, offset_a = offsets(layers), offsets(resps)
    eye = jnp.where(
        lax.broadcasted_iota(jnp.int32, (resps, resps), 0)
        == lax.broadcasted_iota(jnp.int32, (resps, resps), 1),
        1.0,
        0.0,
    ).astype(BF16)
    base_f[...] = jnp.zeros_like(base_f)
    size_f = TAPS * TAPS * layers
    base_f[:, offset_f : offset_f + size_f] = dot_nt(eye, taps_ref[...]).astype(BF16)
    base_a[...] = jnp.zeros_like(base_a)
    group = LANES // math.gcd(LANES, resps)
    for lead in range(0, TAPS * TAPS, group):
        blocks = [
            taps_ref[pl.ds((TAPS * TAPS - 1 - m) * layers, layers), :]
            for m in range(lead, min(lead + group, TAPS * TAPS))
        ]
        begin = offset_a + lead * resps
        base_a[:, begin : begin + len(blocks) * resps] = jnp.concatenate(blocks, axis=1)
    for base, out, offset, depth in (
        (base_f, toeplitz_f, offset_f, layers),
        (base_a, toeplitz_a, offset_a, resps),
    ):
        height, width = base.shape[0], out.shape[1]
        whole = base[...]
        for a in range(HALO):
            begin = offset - a * TAPS * depth
            out[pl.ds(a * height, height), :] = whole[:, begin : begin + width]

    for d in order:
        @pl.when(exists(*d))
        def _():
            for c in range(len(copies(*d))):
                remote(d, c).wait_send()

        @pl.when(exists(-d[0], -d[1]))
        def _():
            for c in range(len(copies(*d))):
                remote(d, c).wait_recv()


def product_kernel(
    dims,
    weight_ref,
    cells_ref,
    own_resid,
    toeplitz_f,
    toeplitz_a,
    own_model,
    halo_model,
    halo_resid,
    halo_cells,
    edges,
    corners,
    predicted_ref,
    gradient_ref,
    padded_f,
    padded_a,
    stack_f,
    stack_a,
    mixed,
):
    tx_count, ty_count, layers, resps, rows, cols = dims
    tall = rows + 2 * HALO

    weights = weight_ref[...].astype(F32)
    cells = cells_ref[:1, :]
    row_of, col_of = cells // cols, cells % cols
    hot = one_hot(col_of, cols)

    total = layers * rows
    thick = HALO * layers
    padded_f[pl.ds(0, thick), LANES : LANES + cols] = halo_model[0]
    padded_f[pl.ds(thick, total), LANES : LANES + cols] = own_model[...]
    padded_f[pl.ds(thick + total, thick), LANES : LANES + cols] = halo_model[1]
    thick_a = HALO * resps
    total_a = resps * rows
    padded_a[pl.ds(thick_a, total_a), LANES : LANES + cols] = own_resid[...]
    for side in range(2):
        other = halo_cells[side][:1]
        values = halo_resid[side].astype(F32)
        first = rows - HALO if side == 0 else 0
        start = 0 if side == 0 else thick_a + total_a
        padded_a[pl.ds(start, thick_a), LANES : LANES + cols] = dot_nt(
            spread_rows(values, other // cols, first, HALO), one_hot(other % cols, cols)
        ).astype(BF16)
    for side in range(2):
        top, mid, low = corners[0, side], edges[side], corners[1, side]
        line_f = jnp.concatenate([top[:, :thick], mid[:, :total], low[:, :thick]], axis=1)
        wide = corners.shape[-1] - thick
        over = wide - thick_a
        line_a = jnp.concatenate(
            [top[:, thick + over :], mid[:, total:], low[:, thick : thick + thick_a]], axis=1
        )
        for line, padded in ((line_f, padded_f), (line_a, padded_a)):
            blank = jnp.zeros((LANES - EDGE, line.shape[1]), F32)
            line = line.astype(F32)
            if side == 0:
                block = jnp.concatenate([blank, line], axis=0).T
                padded[:, :LANES] = block.astype(BF16)
            else:
                block = jnp.concatenate([line, blank], axis=0).T
                padded[:, LANES + cols :] = block.astype(BF16)

    for padded, stack, depth in ((padded_f, stack_f, layers), (padded_a, stack_a, resps)):
        for x in range(tall):
            block = padded[pl.ds(x * depth, depth), :]
            for q in range(TAPS):
                begin = LANES - HALO + q
                stack[pl.ds((x * TAPS + q) * depth, depth), :] = block[:, begin : begin + cols]

    sampled = None
    for h in range(rows // HALO):
        deep = toeplitz_f.shape[1]
        field = dot_nn(toeplitz_f[...], stack_f[pl.ds(h * HALO * TAPS * layers, deep), :])
        high = field.astype(BF16)
        low = (field - high.astype(F32)).astype(BF16)
        spots = dot_nn(high, hot) + dot_nn(low, hot)
        for a in range(HALO):
            term = jnp.where(row_of == h * HALO + a, spots[a * resps : (a + 1) * resps], 0.0)
            sampled = term if sampled is None else sampled + term
    predicted_ref[...] = sampled * weights

    for h in range(rows // HALO):
        deep = toeplitz_a.shape[1]
        grad = dot_nn(toeplitz_a[...], stack_a[pl.ds(h * HALO * TAPS * resps, deep), :])
        for a in range(HALO):
            for t in range(cols // LANES):
                mixed[t, pl.ds(h * HALO + a, layers, stride=rows), :] = grad[
                    a * layers : (a + 1) * layers, t * LANES : (t + 1) * LANES
                ]
    for t in range(cols // LANES):
        gradient_ref[:, t * LANES : (t + 1) * LANES] = mixed[t]


def fused_kernel(dims, *refs):
    arrays, results, scratch = refs[:5], refs[5:7], refs[7:]
    exchange_kernel(dims, *arrays, *scratch[:22])
    product_kernel(dims, *scratch[:11], *results, *scratch[22:])


def shards(tx_count, ty_count, model_pert, station_cells, station_resid, data_weight, kernels):
    layers, rows, cols = model_pert.shape
    resps = kernels.shape[0]
    stations = station_cells.shape[-1]
    dims = (tx_count, ty_count, layers, resps, rows, cols)
    cells, resid, weight = station_cells[0], station_resid[0, 0], data_weight[0, 0]
    model = model_pert.reshape(layers * rows, cols)
    line = (layers + resps) * rows
    thick_a = -(-HALO * resps // LANES) * LANES
    vmem = pl.BlockSpec(memory_space=pltpu.VMEM)
    shape = jax.ShapeDtypeStruct
    copy_count = 2 * 3 + 2 + 4 * 2
    hbm = pl.BlockSpec(memory_space=pltpu.HBM)
    reach = TAPS + HALO - 1
    wide_f, wide_a = reach * TAPS * layers, reach * TAPS * resps
    forward = jnp.transpose(kernels, (2, 3, 1, 0)).reshape(TAPS * TAPS * layers, resps)
    tall = rows + 2 * HALO
    predicted, gradient = pl.pallas_call(
        functools.partial(fused_kernel, dims),
        out_shape=(
            shape((resps, stations), F32),
            shape((layers * rows, cols), F32),
        ),
        in_specs=[hbm] * 5,
        out_specs=(vmem,) * 2,
        scratch_shapes=[
            pltpu.VMEM((resps, stations), jnp.int32),
            pltpu.VMEM((8, stations), jnp.int32),
            pltpu.VMEM((resps * rows, cols), BF16),
            pltpu.VMEM((HALO * resps, wide_f), BF16),
            pltpu.VMEM((HALO * layers, wide_a), BF16),
            pltpu.VMEM((layers * rows, cols), BF16),
            pltpu.VMEM((2, HALO * layers, cols), BF16),
            pltpu.VMEM((2, resps, stations), BF16),
            pltpu.VMEM((2, 8, stations), jnp.int32),
            pltpu.VMEM((2, EDGE, line), BF16),
            pltpu.VMEM((2, 2, EDGE, HALO * layers + thick_a), BF16),
            pltpu.VMEM((1, stations), jnp.int32),
            pltpu.VMEM((resps, stations), BF16),
            pltpu.VMEM((layers * rows, cols), BF16),
            pltpu.VMEM((TAPS * TAPS * layers, resps), BF16),
            pltpu.VMEM((resps, round_up(offsets(layers) + wide_f)), BF16),
            pltpu.VMEM((layers, round_up(offsets(resps) + wide_a)), BF16),
            pltpu.VMEM((resps, stations), BF16),
            pltpu.VMEM((2, EDGE, line), BF16),
            pltpu.SemaphoreType.DMA((5,)),
            pltpu.SemaphoreType.DMA((copy_count,)),
            pltpu.SemaphoreType.DMA((copy_count,)),
            pltpu.VMEM((tall * layers, cols + 2 * LANES), BF16),
            pltpu.VMEM((tall * resps, cols + 2 * LANES), BF16),
            pltpu.VMEM((tall * TAPS * layers, cols), BF16),
            pltpu.VMEM((tall * TAPS * resps, cols), BF16),
            pltpu.VMEM((cols // LANES, layers * rows, LANES), F32),
        ],
        compiler_params=pltpu.CompilerParams(
            collective_id=0, has_side_effects=True, vmem_limit_bytes=60 * 2**20
        ),
    )(cells, resid, weight, model, forward)
    return predicted[None, None], gradient.reshape(layers, rows, cols)


def solution(mesh):
    placed = (
        P("surveys", "tx", "ty"),
        P(("surveys", "tx"), "ty", None),
        P(("surveys", "tx"), "ty", None, None),
        P(("surveys", "tx"), "ty", None, None),
        P(),
    )
    return jax.shard_map(
        functools.partial(shards, mesh.shape["tx"], mesh.shape["ty"]),
        mesh=mesh,
        in_specs=placed,
        out_specs=(P(("surveys", "tx"), "ty", None, None), P("surveys", "tx", "ty")),
        check_vma=False,
    )
```

```python
import functools
import math

import jax
import jax.numpy as jnp
from jax import lax
from jax.experimental import pallas as pl
from jax.experimental.pallas import tpu as pltpu
from jax.sharding import PartitionSpec as P

HALO = 4
TAPS = 9
LANES = 128
EDGE = 16
BF16 = jnp.bfloat16
F32 = jnp.float32
NT = (((1,), (1,)), ((), ()))


def dot_nt(a, b):
    return lax.dot_general(a, b, NT, preferred_element_type=F32)


def dot_nn(a, b):
    return jnp.dot(a, b, preferred_element_type=F32)


def spread_rows(values, station_rows, first, count):
    return jnp.concatenate(
        [jnp.where(station_rows == first + x, values, 0.0).astype(BF16) for x in range(count)],
        axis=0,
    )


def one_hot(ids, count, first=0):
    spot = lax.broadcasted_iota(jnp.int32, (count, ids.shape[1]), 0) + first
    return jnp.where(spot == ids, 1.0, 0.0).astype(BF16)


def round_up(size):
    return -(-size // LANES) * LANES


def offsets(depth):
    return round_up((HALO - 1) * TAPS * depth)


def exchange_kernel(
    dims,
    cells_hbm,
    resid_hbm,
    weight_hbm,
    model_hbm,
    taps_hbm,
    weight_ref,
    send_cells,
    own_resid,
    toeplitz_f,
    toeplitz_a,
    own_model,
    halo_model,
    halo_resid,
    halo_cells,
    edges,
    corners,
    cells_ref,
    resid_ref,
    model_ref,
    taps_ref,
    base_f,
    base_a,
    send_resid,
    send_edges,
    load_sems,
    send_sems,
    recv_sems,
):
    tx_count, ty_count, layers, resps, rows, cols = dims
    tx, ty = lax.axis_index("tx"), lax.axis_index("ty")
    has = {-1: tx > 0, 1: tx < tx_count - 1}
    has_col = {-1: ty > 0, 1: ty < ty_count - 1}
    around = [(dx, dy) for dx in (-1, 0, 1) for dy in (-1, 0, 1) if (dx, dy) != (0, 0)]

    def exists(dx, dy):
        ok = None
        for part in ([has[dx]] if dx else []) + ([has_col[dy]] if dy else []):
            ok = part if ok is None else jnp.logical_and(ok, part)
        return ok

    loads = [
        pltpu.make_async_copy(src, dst, load_sems.at[n])
        for n, (src, dst) in enumerate(
            (
                (cells_hbm, cells_ref),
                (resid_hbm, resid_ref),
                (weight_hbm, weight_ref),
                (model_hbm, model_ref),
                (taps_hbm, taps_ref),
            )
        )
    ]
    for load in loads:
        load.start()
    barrier = pltpu.get_barrier_semaphore()
    for dx, dy in around:
        @pl.when(exists(dx, dy))
        def _():
            pl.semaphore_signal(
                barrier,
                inc=1,
                device_id={"tx": tx + dx, "ty": ty + dy},
                device_id_type=pl.DeviceIdType.MESH,
            )

    for side, dx in enumerate((-1, 1)):
        @pl.when(jnp.logical_not(has[dx]))
        def _():
            halo_model[side] = jnp.zeros(halo_model.shape[1:], BF16)
            halo_resid[side] = jnp.zeros(halo_resid.shape[1:], BF16)
            halo_cells[side] = jnp.zeros(halo_cells.shape[1:], jnp.int32)
    for side, dy in enumerate((-1, 1)):
        @pl.when(jnp.logical_not(has_col[dy]))
        def _():
            edges[side] = jnp.zeros(edges.shape[1:], BF16)
    for vert, dx in enumerate((-1, 1)):
        for side, dy in enumerate((-1, 1)):
            @pl.when(jnp.logical_not(exists(dx, dy)))
            def _():
                corners[vert, side] = jnp.zeros(corners.shape[2:], BF16)

    for load in loads[:3]:
        load.wait()
    weighted = resid_ref[...].astype(F32) * weight_ref[...].astype(F32)
    send_resid[...] = weighted.astype(BF16)
    send_cells[...] = jnp.broadcast_to(cells_ref[...], send_cells.shape)

    total = layers * rows
    loads[3].wait()
    to = lax.broadcasted_iota(jnp.int32, (total, total), 0)
    frm = lax.broadcasted_iota(jnp.int32, (total, total), 1)
    source = (to % layers) * rows + to // layers
    perm = jnp.where(frm == source, 1.0, 0.0).astype(BF16)
    own_model[...] = dot_nn(perm, model_ref[...]).astype(BF16)

    spans = [
        1 + both[-1].astype(jnp.int32) + both[1].astype(jnp.int32) for both in (has, has_col)
    ]
    pl.semaphore_wait(barrier, spans[0] * spans[1] - 1)

    thick = HALO * layers
    wide = corners.shape[-1] - thick

    def copies(dx, dy):
        pairs = []
        if dy == 0:
            mine = 1 if dx == -1 else 0
            start = 0 if dx == -1 else total - thick
            pairs.append((own_model.at[pl.ds(start, thick)], halo_model.at[mine]))
            pairs.append((send_resid, halo_resid.at[mine]))
            pairs.append((send_cells, halo_cells.at[mine]))
        elif dx == 0:
            mine = 1 if dy == -1 else 0
            pairs.append((send_edges.at[1 - mine], edges.at[mine]))
        else:
            vert, side = (1 if dx == -1 else 0), (1 if dy == -1 else 0)
            start = 0 if dx == -1 else total - thick
            start_resid = total if dx == -1 else send_edges.shape[-1] - wide
            src = send_edges.at[1 - side]
            dst = corners.at[vert, side]
            pairs.append((src.at[:, pl.ds(start, thick)], dst.at[:, pl.ds(0, thick)]))
            pairs.append((src.at[:, pl.ds(start_resid, wide)], dst.at[:, pl.ds(thick, wide)]))
        return pairs

    number = {}
    for d in around:
        for c in range(len(copies(*d))):
            number[d, c] = len(number)

    def remote(d, c):
        src, dst = copies(*d)[c]
        return pltpu.make_async_remote_copy(
            src_ref=src,
            dst_ref=dst,
            send_sem=send_sems.at[number[d, c]],
            recv_sem=recv_sems.at[number[d, c]],
            device_id={"tx": tx + d[0], "ty": ty + d[1]},
            device_id_type=pl.DeviceIdType.MESH,
        )

    order = sorted(around, key=lambda d: abs(d[1]))

    def start(d):
        @pl.when(exists(*d))
        def _():
            for c in range(len(copies(*d))):
                remote(d, c).start()

    for d in order[:2]:
        start(d)

    cells = cells_ref[...]
    row_of, col_of = cells // cols, cells % cols
    spread = spread_rows(weighted, row_of, 0, rows)
    near = lax.broadcasted_iota(jnp.int32, (EDGE, cols), 0)
    lane = lax.broadcasted_iota(jnp.int32, (EDGE, cols), 1)
    for side, first in enumerate((0, cols - EDGE)):
        pick = jnp.where(lane == near + first, 1.0, 0.0).astype(BF16)
        send_edges[side, :, :total] = dot_nt(pick, own_model[...]).astype(BF16)
        send_edges[side, :, total:] = dot_nt(one_hot(col_of, EDGE, first), spread).astype(BF16)

    for d in order[2:]:
        start(d)

    own_resid[...] = dot_nt(spread, one_hot(col_of, cols)).astype(BF16)

    loads[4].wait()
    offset_f, offset_a = offsets(layers), offsets(resps)
    eye = jnp.where(
        lax.broadcasted_iota(jnp.int32, (resps, resps), 0)
        == lax.broadcasted_iota(jnp.int32, (resps, resps), 1),
        1.0,
        0.0,
    ).astype(BF16)
    base_f[...] = jnp.zeros_like(base_f)
    size_f = TAPS * TAPS * layers
    base_f[:, offset_f : offset_f + size_f] = dot_nt(eye, taps_ref[...]).astype(BF16)
    base_a[...] = jnp.zeros_like(base_a)
    group = LANES // math.gcd(LANES, resps)
    for lead in range(0, TAPS * TAPS, group):
        blocks = [
            taps_ref[pl.ds((TAPS * TAPS - 1 - m) * layers, layers), :]
            for m in range(lead, min(lead + group, TAPS * TAPS))
        ]
        begin = offset_a + lead * resps
        base_a[:, begin : begin + len(blocks) * resps] = jnp.concatenate(blocks, axis=1)
    for base, out, offset, depth in (
        (base_f, toeplitz_f, offset_f, layers),
        (base_a, toeplitz_a, offset_a, resps),
    ):
        height, width = base.shape[0], out.shape[1]
        whole = base[...]
        for a in range(HALO):
            begin = offset - a * TAPS * depth
            out[pl.ds(a * height, height), :] = whole[:, begin : begin + width]

    def arrive(chosen):
        for d in chosen:
            @pl.when(exists(-d[0], -d[1]))
            def _():
                for c in range(len(copies(*d))):
                    remote(d, c).wait_recv()

    def finish():
        for d in order:
            @pl.when(exists(*d))
            def _():
                for c in range(len(copies(*d))):
                    remote(d, c).wait_send()

    beside = [d for d in order if d[0] == 0]
    across = [d for d in order if d[0] != 0]
    return functools.partial(arrive, beside), functools.partial(arrive, across), finish


def product_kernel(
    dims,
    arrive_beside,
    arrive_across,
    weight_ref,
    cells_ref,
    own_resid,
    toeplitz_f,
    toeplitz_a,
    own_model,
    halo_model,
    halo_resid,
    halo_cells,
    edges,
    corners,
    predicted_ref,
    gradient_ref,
    padded_f,
    padded_a,
    stack_f,
    stack_a,
    mixed,
):
    tx_count, ty_count, layers, resps, rows, cols = dims
    tall = rows + 2 * HALO

    weights = weight_ref[...].astype(F32)
    cells = cells_ref[:1, :]
    row_of, col_of = cells // cols, cells % cols
    hot = one_hot(col_of, cols)

    total = layers * rows
    thick = HALO * layers
    thick_a = HALO * resps
    total_a = resps * rows
    centre = slice(LANES, LANES + cols)
    wide = corners.shape[-1] - thick
    over = wide - thick_a

    def put_columns(line, padded, start, side):
        blank = jnp.zeros((LANES - EDGE, line.shape[1]), F32)
        line = line.astype(F32)
        if side == 0:
            block = jnp.concatenate([blank, line], axis=0).T
            padded[pl.ds(start, block.shape[0]), :LANES] = block.astype(BF16)
        else:
            block = jnp.concatenate([line, blank], axis=0).T
            padded[pl.ds(start, block.shape[0]), LANES + cols :] = block.astype(BF16)

    def shift(rows_of):
        for padded, stack, depth in ((padded_f, stack_f, layers), (padded_a, stack_a, resps)):
            for x in rows_of:
                block = padded[pl.ds(x * depth, depth), :]
                for q in range(TAPS):
                    begin = LANES - HALO + q
                    stack[pl.ds((x * TAPS + q) * depth, depth), :] = block[:, begin : begin + cols]

    def products(groups, sampled):
        for h in groups:
            deep = toeplitz_f.shape[1]
            field = dot_nn(toeplitz_f[...], stack_f[pl.ds(h * HALO * TAPS * layers, deep), :])
            high = field.astype(BF16)
            low = (field - high.astype(F32)).astype(BF16)
            spots = dot_nn(high, hot) + dot_nn(low, hot)
            for a in range(HALO):
                term = jnp.where(
                    row_of == h * HALO + a, spots[a * resps : (a + 1) * resps], 0.0
                )
                sampled = term if sampled is None else sampled + term
            deep = toeplitz_a.shape[1]
            grad = dot_nn(toeplitz_a[...], stack_a[pl.ds(h * HALO * TAPS * resps, deep), :])
            for a in range(HALO):
                for t in range(cols // LANES):
                    mixed[t, pl.ds(h * HALO + a, layers, stride=rows), :] = grad[
                        a * layers : (a + 1) * layers, t * LANES : (t + 1) * LANES
                    ]
        return sampled

    padded_f[pl.ds(thick, total), centre] = own_model[...]
    padded_a[pl.ds(thick_a, total_a), centre] = own_resid[...]
    arrive_beside()
    for side in range(2):
        put_columns(edges[side][:, :total], padded_f, thick, side)
        put_columns(edges[side][:, total:], padded_a, thick_a, side)
    shift(range(HALO, HALO + rows))
    last = rows // HALO - 1
    sampled = products(range(1, last), None)

    arrive_across()
    for vert in range(2):
        start_f = 0 if vert == 0 else thick + total
        start_a = 0 if vert == 0 else thick_a + total_a
        padded_f[pl.ds(start_f, thick), centre] = halo_model[vert]
        other = halo_cells[vert][:1]
        values = halo_resid[vert].astype(F32)
        first = rows - HALO if vert == 0 else 0
        padded_a[pl.ds(start_a, thick_a), centre] = dot_nt(
            spread_rows(values, other // cols, first, HALO), one_hot(other % cols, cols)
        ).astype(BF16)
        for side in range(2):
            corner = corners[vert, side]
            begin = thick + over if vert == 0 else thick
            put_columns(corner[:, :thick], padded_f, start_f, side)
            put_columns(corner[:, begin : begin + thick_a], padded_a, start_a, side)
    shift([*range(HALO), *range(HALO + rows, tall)])
    sampled = products([0, last], sampled)
    predicted_ref[...] = sampled * weights
    for t in range(cols // LANES):
        gradient_ref[:, t * LANES : (t + 1) * LANES] = mixed[t]


def fused_kernel(dims, *refs):
    arrays, results, scratch = refs[:5], refs[5:7], refs[7:]
    beside, across, finish = exchange_kernel(dims, *arrays, *scratch[:22])
    product_kernel(dims, beside, across, *scratch[:11], *results, *scratch[22:])
    finish()


def shards(tx_count, ty_count, model_pert, station_cells, station_resid, data_weight, kernels):
    layers, rows, cols = model_pert.shape
    resps = kernels.shape[0]
    stations = station_cells.shape[-1]
    dims = (tx_count, ty_count, layers, resps, rows, cols)
    cells, resid, weight = station_cells[0], station_resid[0, 0], data_weight[0, 0]
    model = model_pert.reshape(layers * rows, cols)
    line = (layers + resps) * rows
    thick_a = -(-HALO * resps // LANES) * LANES
    vmem = pl.BlockSpec(memory_space=pltpu.VMEM)
    shape = jax.ShapeDtypeStruct
    copy_count = 2 * 3 + 2 + 4 * 2
    hbm = pl.BlockSpec(memory_space=pltpu.HBM)
    reach = TAPS + HALO - 1
    wide_f, wide_a = reach * TAPS * layers, reach * TAPS * resps
    forward = jnp.transpose(kernels, (2, 3, 1, 0)).reshape(TAPS * TAPS * layers, resps)
    tall = rows + 2 * HALO
    predicted, gradient = pl.pallas_call(
        functools.partial(fused_kernel, dims),
        out_shape=(
            shape((resps, stations), F32),
            shape((layers * rows, cols), F32),
        ),
        in_specs=[hbm] * 5,
        out_specs=(vmem,) * 2,
        scratch_shapes=[
            pltpu.VMEM((resps, stations), jnp.int32),
            pltpu.VMEM((8, stations), jnp.int32),
            pltpu.VMEM((resps * rows, cols), BF16),
            pltpu.VMEM((HALO * resps, wide_f), BF16),
            pltpu.VMEM((HALO * layers, wide_a), BF16),
            pltpu.VMEM((layers * rows, cols), BF16),
            pltpu.VMEM((2, HALO * layers, cols), BF16),
            pltpu.VMEM((2, resps, stations), BF16),
            pltpu.VMEM((2, 8, stations), jnp.int32),
            pltpu.VMEM((2, EDGE, line), BF16),
            pltpu.VMEM((2, 2, EDGE, HALO * layers + thick_a), BF16),
            pltpu.VMEM((1, stations), jnp.int32),
            pltpu.VMEM((resps, stations), BF16),
            pltpu.VMEM((layers * rows, cols), BF16),
            pltpu.VMEM((TAPS * TAPS * layers, resps), BF16),
            pltpu.VMEM((resps, round_up(offsets(layers) + wide_f)), BF16),
            pltpu.VMEM((layers, round_up(offsets(resps) + wide_a)), BF16),
            pltpu.VMEM((resps, stations), BF16),
            pltpu.VMEM((2, EDGE, line), BF16),
            pltpu.SemaphoreType.DMA((5,)),
            pltpu.SemaphoreType.DMA((copy_count,)),
            pltpu.SemaphoreType.DMA((copy_count,)),
            pltpu.VMEM((tall * layers, cols + 2 * LANES), BF16),
            pltpu.VMEM((tall * resps, cols + 2 * LANES), BF16),
            pltpu.VMEM((tall * TAPS * layers, cols), BF16),
            pltpu.VMEM((tall * TAPS * resps, cols), BF16),
            pltpu.VMEM((cols // LANES, layers * rows, LANES), F32),
        ],
        compiler_params=pltpu.CompilerParams(
            collective_id=0, has_side_effects=True, vmem_limit_bytes=60 * 2**20
        ),
    )(cells, resid, weight, model, forward)
    return predicted[None, None], gradient.reshape(layers, rows, cols)


def solution(mesh):
    placed = (
        P("surveys", "tx", "ty"),
        P(("surveys", "tx"), "ty", None),
        P(("surveys", "tx"), "ty", None, None),
        P(("surveys", "tx"), "ty", None, None),
        P(),
    )
    return jax.shard_map(
        functools.partial(shards, mesh.shape["tx"], mesh.shape["ty"]),
        mesh=mesh,
        in_specs=placed,
        out_specs=(P(("surveys", "tx"), "ty", None, None), P("surveys", "tx", "ty")),
        check_vma=False,
    )
```
